32 devices in a mesh: ctx: 8 (over z, y), head: 4 (over x, core).
Axes of the slice: x: 2, y: 2, z: 4, core: 2. Of those that a mesh axis runs over, the one named last changes fastest.
Arguments:
- lin_q: bfloat16 [1024, 2048], P('ctx', 'head'), may hold values from -5 to 5
- lin_k: bfloat16 [1024, 2048], P('ctx', 'head'), may hold values from -5 to 5
- lin_v: bfloat16 [1024, 2048], P('ctx', 'head'), may hold values from -13 to 13
- win_q: bfloat16 [1024, 2048], P('ctx', 'head'), may hold values from -5 to 5
- win_k: bfloat16 [1024, 2048], P('ctx', 'head'), may hold values from -5 to 5
- win_v: bfloat16 [1024, 2048], P('ctx', 'head'), may hold values from -5 to 5
- grad_out: bfloat16 [1024, 2048], P('ctx', 'head'), may hold values from -5 to 5
Outputs:
- mixed: bfloat16 [1024, 2048], P('ctx', 'head')
- grad_lin_q: bfloat16 [1024, 2048], P('ctx', 'head')
- grad_lin_k: bfloat16 [1024, 2048], P('ctx', 'head')
- grad_lin_v: bfloat16 [1024, 2048], P('ctx', 'head')
- grad_win_q: bfloat16 [1024, 2048], P('ctx', 'head')
- grad_win_k: bfloat16 [1024, 2048], P('ctx', 'head')
- grad_win_v: bfloat16 [1024, 2048], P('ctx', 'head')
The draws below stay inside these ranges and needn't reach their ends.
All inputs are finite; a program needn't handle non-finite values.
Results may differ from the reference program's by a relative error of at most 0.0084.
Values may be sent and summed in bfloat16 or wider, within the bound.
A program may use at most 64 MiB of HBM per device.

```python
import math
import jax
import jax.numpy as jnp
from jax import lax

HD = 128
WIN = 512
TOK_DEV = 128
HEADS = 16
TOKENS = 1024


def drawn_pair(key):
    base = jax.random.fold_in(key, 17)
    key_query, key_keys = jax.random.split(base, 2)
    shape = (TOKENS, HEADS * HD)
    query = jnp.clip(1.4 * jax.random.normal(key_query, shape, jnp.float32), -5.0, 5.0)
    keys = jnp.clip(1.4 * jax.random.normal(key_keys, shape, jnp.float32), -5.0, 5.0)
    return (query, keys)


def draw_win_q(key, part):
    return drawn_pair(key)[0].astype(jnp.bfloat16)


def draw_win_k(key, part):
    return drawn_pair(key)[1].astype(jnp.bfloat16)


def draw_lin_v(key, part):
    base = jax.random.fold_in(key, 29)
    key_body, key_spread = jax.random.split(base, 2)
    columns = HEADS * HD
    feature = jnp.arange(columns, dtype=jnp.float32) / columns
    values = jnp.clip(jax.random.normal(key_body, (TOKENS, columns), jnp.float32), -4.0, 4.0)
    rising = 0.5
    offset = -0.5
    spread = jax.random.uniform(key_spread, (columns,), jnp.float32, 0.0, 0.5)
    column_scale = 10.0 ** (rising * feature + spread + offset)
    return (values * column_scale[None, :]).astype(jnp.bfloat16)


def steps_of(key, shape, shards, low, largest):
    factor_of, own = 1.0, jax.random.fold_in(key, 6)
    for dim, parts in shards:
        steps = jnp.exp(jax.random.uniform(jax.random.fold_in(own, dim), (parts,), jnp.float32, low / len(shards), largest / len(shards)))
        factor_of = factor_of * jnp.repeat(steps, shape[dim] // parts).reshape([-1 if axis == dim else 1 for axis in range(len(shape))])
    return factor_of


def bell_draw(rng, extent, width, reach, shards=(), held_as=jnp.bfloat16):
    values = width * jax.random.normal(rng, extent, jnp.float32)
    if shards:
        values = values * steps_of(rng, extent, shards, -0.22, 0.18)
    return jnp.clip(values, -reach, reach).astype(held_as)


def setup_inputs(seed: int = 0) -> dict:
    key_list = jax.random.split(jax.random.key(seed), 8)
    lin_q = bell_draw(key_list[0], (TOKENS, HEADS * HD), 1.0, 5.0, ((0, 8), (1, 4)))
    lin_k = bell_draw(key_list[1], (TOKENS, HEADS * HD), 1.0, 5.0, ((0, 8), (1, 4)))
    lin_v = draw_lin_v(jax.random.fold_in(key_list[7], 71), 0)
    win_q = draw_win_q(jax.random.fold_in(key_list[7], 71), 0)
    win_k = draw_win_k(jax.random.fold_in(key_list[7], 71), 0)
    win_v = bell_draw(key_list[5], (TOKENS, HEADS * HD), 1.0, 5.0, ((0, 8), (1, 4)))
    grad_out = bell_draw(key_list[6], (TOKENS, HEADS * HD), 1.0, 5.0, ((0, 8), (1, 4)))
    return dict(lin_q=lin_q, lin_k=lin_k, lin_v=lin_v, win_q=win_q, win_k=win_k, win_v=win_v, grad_out=grad_out)


PRECISE = lax.Precision.HIGHEST
NORM_EPS = 1e-05

def split_blocks(array, block_rows):
    return array.reshape((array.shape[0] // block_rows, block_rows) + array.shape[1:])

def block_states(left, right, block_rows):
    first_part = split_blocks(left.astype(jnp.float32), block_rows)
    second_part = split_blocks(right.astype(jnp.float32), block_rows)
    return jnp.einsum('bshd,bshe->bhde', first_part, second_part, precision=PRECISE)

def exclusive(states, reverse):
    empty = jnp.zeros_like(states[:1])
    if reverse:
        running = jnp.cumsum(states[::-1], axis=0)[::-1]
        return jnp.concatenate([running[1:], empty], axis=0)
    running = jnp.cumsum(states, axis=0)
    return jnp.concatenate([empty, running[:-1]], axis=0)

def causal_rows(block_rows):
    positions = jnp.arange(block_rows, dtype=jnp.int32)
    return positions[:, None] >= positions[None, :]

def linear_forward(query, keys, values, before_blocks, block_rows):
    causal = causal_rows(block_rows)

    def per_block(pieces):
        query_f = pieces[0].astype(jnp.float32)
        keys_f = pieces[1].astype(jnp.float32)
        values_f = pieces[2].astype(jnp.float32)
        scores = jnp.einsum('thd,shd->hts', query_f, keys_f, precision=PRECISE)
        scores = jnp.where(causal[None], scores, 0.0)
        inner = jnp.einsum('hts,shd->thd', scores, values_f, precision=PRECISE)
        return inner + jnp.einsum('thd,hde->the', query_f, pieces[3], precision=PRECISE)
    result = lax.map(per_block, (split_blocks(query, block_rows), split_blocks(keys, block_rows), split_blocks(values, block_rows), before_blocks))
    return result.reshape(query.shape)

def linear_backward(query, keys, values, cotangent, before_blocks, after_blocks, block_rows):
    causal = causal_rows(block_rows)

    def per_block(pieces):
        query_f = pieces[0].astype(jnp.float32)
        keys_f = pieces[1].astype(jnp.float32)
        values_f = pieces[2].astype(jnp.float32)
        upstream = pieces[3].astype(jnp.float32)
        scores = jnp.einsum('thd,shd->hts', query_f, keys_f, precision=PRECISE)
        scores = jnp.where(causal[None], scores, 0.0)
        dprobs = jnp.einsum('the,she->hts', upstream, values_f, precision=PRECISE)
        dprobs = jnp.where(causal[None], dprobs, 0.0)
        query_grad = jnp.einsum('hts,shd->thd', dprobs, keys_f, precision=PRECISE)
        query_grad = query_grad + jnp.einsum('the,hde->thd', upstream, pieces[4], precision=PRECISE)
        key_grad = jnp.einsum('hts,thd->shd', dprobs, query_f, precision=PRECISE)
        key_grad = key_grad + jnp.einsum('she,hde->shd', values_f, pieces[5], precision=PRECISE)
        value_grad = jnp.einsum('hts,the->she', scores, upstream, precision=PRECISE)
        value_grad = value_grad + jnp.einsum('shd,hde->she', keys_f, pieces[5], precision=PRECISE)
        return (query_grad, key_grad, value_grad)
    grads = lax.map(per_block, (split_blocks(query, block_rows), split_blocks(keys, block_rows), split_blocks(values, block_rows), split_blocks(cotangent, block_rows), before_blocks, after_blocks))
    return tuple((item.reshape(query.shape) for item in grads))

def query_head(query, keys, values, upstream, first_pos):
    row_count = query.shape[0]
    ext_count = keys.shape[0]
    window = ext_count - row_count
    score_scale = 1.0 / math.sqrt(query.shape[1])
    keys_f = keys.astype(jnp.float32)
    values_f = values.astype(jnp.float32)
    scores = jnp.einsum('td,sd->ts', query.astype(jnp.float32), keys_f, precision=PRECISE) * score_scale
    query_pos = first_pos + jnp.arange(row_count, dtype=jnp.int32)
    key_pos = first_pos - window + jnp.arange(ext_count, dtype=jnp.int32)
    allowed = (key_pos[None, :] >= 0) & (key_pos[None, :] <= query_pos[:, None]) & (key_pos[None, :] > query_pos[:, None] - window)
    scores = jnp.where(allowed, scores, -jnp.inf)
    row_max = lax.optimization_barrier(jnp.max(scores, axis=1, keepdims=True))
    log_total = row_max[:, 0] + jnp.log(lax.optimization_barrier(jnp.sum(jnp.exp(scores - row_max), axis=1)))
    probs = jnp.exp(scores - log_total[:, None])
    weights_low = probs.astype(jnp.bfloat16)
    output = jnp.einsum('ts,sd->td', weights_low.astype(jnp.float32), values_f, precision=PRECISE)
    dprobs = jnp.einsum('td,sd->ts', upstream.astype(jnp.float32), values_f, precision=PRECISE)
    row_dot = lax.optimization_barrier(jnp.sum(probs * dprobs, axis=1))
    dscores = (probs * (dprobs - row_dot[:, None]) * score_scale).astype(jnp.bfloat16)
    query_grad = jnp.einsum('ts,sd->td', dscores.astype(jnp.float32), keys_f, precision=PRECISE)
    return (output, query_grad, log_total, row_dot)

def key_head(query, upstream, totals, dots, keys, values, first_pos, total_rows):
    row_count = keys.shape[0]
    ext_count = query.shape[0]
    window = ext_count - row_count
    score_scale = 1.0 / math.sqrt(query.shape[1])
    query_f = query.astype(jnp.float32)
    upstream_f = upstream.astype(jnp.float32)
    scores = jnp.einsum('td,sd->ts', query_f, keys.astype(jnp.float32), precision=PRECISE) * score_scale
    query_pos = first_pos + jnp.arange(ext_count, dtype=jnp.int32)
    key_pos = first_pos + jnp.arange(row_count, dtype=jnp.int32)
    allowed = (query_pos[:, None] < total_rows) & (key_pos[None, :] <= query_pos[:, None]) & (key_pos[None, :] > query_pos[:, None] - window)
    probs = jnp.where(allowed, jnp.exp(scores - totals[:, None]), 0.0)
    weights_low = probs.astype(jnp.bfloat16)
    dprobs = jnp.einsum('td,sd->ts', upstream_f, values.astype(jnp.float32), precision=PRECISE)
    dscores = (probs * (dprobs - dots[:, None]) * score_scale).astype(jnp.bfloat16)
    key_grad = jnp.einsum('ts,td->sd', dscores.astype(jnp.float32), query_f, precision=PRECISE)
    value_grad = jnp.einsum('ts,td->sd', weights_low.astype(jnp.float32), upstream_f, precision=PRECISE)
    return (key_grad, value_grad)

def reference(lin_q, lin_k, lin_v, win_q, win_k, win_v, grad_out):
    shaped = (TOKENS, HEADS, HD)
    flat = (TOKENS, HEADS * HD)
    lin_query = lin_q.reshape(shaped)
    lin_key = lin_k.reshape(shaped)
    lin_value = lin_v.reshape(shaped)
    before_blocks = exclusive(block_states(lin_key, lin_value, TOK_DEV), False)
    lin_out = linear_forward(lin_query, lin_key, lin_value, before_blocks, TOK_DEV)
    upstream = grad_out.reshape(shaped).astype(jnp.float32)
    features = HEADS * HD
    square_sum = lax.optimization_barrier(jnp.sum(lin_out * lin_out, axis=(1, 2)))
    cross_sum = lax.optimization_barrier(jnp.sum(upstream * lin_out, axis=(1, 2)))
    inv_rms = lax.rsqrt(square_sum / features + NORM_EPS)
    lin_dout = (inv_rms[:, None, None] * upstream - lin_out * (inv_rms ** 3 * cross_sum / features)[:, None, None]).astype(jnp.bfloat16)
    after_blocks = exclusive(block_states(lin_query, lin_dout, TOK_DEV), True)
    grad_q, grad_k, grad_v = linear_backward(lin_query, lin_key, lin_value, lin_dout, before_blocks, after_blocks, TOK_DEV)
    win_query = win_q.reshape(shaped)
    win_key = win_k.reshape(shaped)
    win_value = win_v.reshape(shaped)
    cotangent = grad_out.reshape(shaped)
    padding = jnp.zeros((WIN, HEADS, HD), jnp.bfloat16)
    key_pad = jnp.concatenate([padding, win_key], axis=0)
    value_pad = jnp.concatenate([padding, win_value], axis=0)
    query_pad = jnp.concatenate([win_query, padding], axis=0)
    upstream_pad = jnp.concatenate([cotangent, padding], axis=0)
    block_index = jnp.arange(TOKENS // TOK_DEV, dtype=jnp.int32)

    def query_block(block):
        first_pos = (block * TOK_DEV).astype(jnp.int32)
        pieces = (lax.dynamic_slice_in_dim(win_query, first_pos, TOK_DEV, 0), lax.dynamic_slice_in_dim(key_pad, first_pos, WIN + TOK_DEV, 0), lax.dynamic_slice_in_dim(value_pad, first_pos, WIN + TOK_DEV, 0), lax.dynamic_slice_in_dim(cotangent, first_pos, TOK_DEV, 0))
        mapped = jax.vmap(lambda a, b, c, d: query_head(a, b, c, d, first_pos), in_axes=1, out_axes=(1, 1, 0, 0))
        return mapped(*pieces)
    win_out, win_dq, log_total, row_dot = lax.map(query_block, block_index)
    win_out = win_out.reshape(shaped)
    win_dq = win_dq.reshape(shaped)
    stat_pad = jnp.zeros((HEADS, WIN), jnp.float32)
    total_all = jnp.concatenate([jnp.moveaxis(log_total, 0, 1).reshape(HEADS, TOKENS), stat_pad], axis=1)
    dot_all = jnp.concatenate([jnp.moveaxis(row_dot, 0, 1).reshape(HEADS, TOKENS), stat_pad], axis=1)

    def key_block(block):
        first_pos = (block * TOK_DEV).astype(jnp.int32)
        pieces = (lax.dynamic_slice_in_dim(query_pad, first_pos, WIN + TOK_DEV, 0), lax.dynamic_slice_in_dim(upstream_pad, first_pos, WIN + TOK_DEV, 0), lax.dynamic_slice_in_dim(total_all, first_pos, WIN + TOK_DEV, 1), lax.dynamic_slice_in_dim(dot_all, first_pos, WIN + TOK_DEV, 1), lax.dynamic_slice_in_dim(win_key, first_pos, TOK_DEV, 0), lax.dynamic_slice_in_dim(win_value, first_pos, TOK_DEV, 0))
        mapped = jax.vmap(lambda a, b, c, d, e, f: key_head(a, b, c, d, e, f, first_pos, TOKENS), in_axes=(1, 1, 0, 0, 1, 1), out_axes=(1, 1))
        return mapped(*pieces)
    win_dk, win_dv = lax.map(key_block, block_index)
    mixed = (lin_out * inv_rms[:, None, None] + win_out).astype(jnp.bfloat16).reshape(flat)
    return (mixed, grad_q.astype(jnp.bfloat16).reshape(flat), grad_k.astype(jnp.bfloat16).reshape(flat), grad_v.astype(jnp.bfloat16).reshape(flat), win_dq.astype(jnp.bfloat16).reshape(flat), win_dk.astype(jnp.bfloat16).reshape(flat), win_dv.astype(jnp.bfloat16).reshape(flat))
```

```python
from functools import partial
import math

import jax
import jax.numpy as jnp
from jax import lax
from jax.experimental import pallas as pl
from jax.experimental.pallas import tpu as pltpu
from jax.sharding import PartitionSpec as P

HD = 128
WIN = 512
NORM_EPS = 1e-05
NEG = -1e30
MESH = pl.DeviceIdType.MESH
F32 = jnp.float32
BF16 = jnp.bfloat16

IN_NAMES = ("lq", "lk", "lv", "wq", "wk", "wv", "go")
OUT_NAMES = ("mixed", "glq", "glk", "glv", "gwq", "gwk", "gwv")


def dot_nn(a, b):
    return lax.dot_general(a, b, (((1,), (0,)), ((), ())), preferred_element_type=F32)


def dot_nt(a, b):
    return lax.dot_general(a, b, (((1,), (1,)), ((), ())), preferred_element_type=F32)


def dot_tn(a, b):
    return lax.dot_general(a, b, (((0,), (0,)), ((), ())), preferred_element_type=F32)


def repeat(low, high, step):
    if high - low <= 16:
        for k in range(low, high):
            step(k)
    else:

        def body(k, carry):
            step(k)
            return carry

        lax.fori_loop(low, high, body, 0)


def owner_count(n, state_rows):
    owners = 1
    while owners * 2 <= n and state_rows % (owners * 2 * 16) == 0:
        owners *= 2
    return owners


def kernel(n, hn, owners, span, names, *refs):
    r = dict(zip(names, refs))
    rows, cols = r["lq"].shape
    heads = cols // HD
    me = lax.axis_index("ctx")
    hme = lax.axis_index("head")
    piece = heads * HD // owners
    scale = 1.0 / math.sqrt(HD)
    features = cols * hn
    col = [slice(h * HD, (h + 1) * HD) for h in range(heads)]

    def around(k):
        return lax.rem(me + k, n)

    def remote(src, dst, send, recv, target, axis="ctx"):
        return pltpu.make_async_remote_copy(
            src_ref=src, dst_ref=dst, send_sem=send, recv_sem=recv,
            device_id={axis: target}, device_id_type=MESH,
        )

    barrier = pltpu.get_barrier_semaphore()

    def greet(k):
        pl.semaphore_signal(barrier, inc=1, device_id={"ctx": around(k)}, device_id_type=MESH)

    repeat(1, n, greet)
    for k in range(1, hn):
        pl.semaphore_signal(
            barrier, inc=1, device_id={"head": lax.rem(hme + k, hn)}, device_id_type=MESH
        )

    def rows_of(owner):
        return pl.ds(pl.multiple_of(owner * piece, piece), piece)

    def state_copy(which, k):
        target = around(k)
        return remote(
            r[which + "_own"].at[rows_of(target)], r[which + "_got"].at[me],
            r[which + "_s1"].at[target], r[which + "_r1"].at[me], target,
        )

    def total_copy(which, k):
        target = around(k)
        return remote(
            r[which + "_sums"].at[target], r[which + "_all"].at[rows_of(me)],
            r[which + "_s2"].at[target], r[which + "_r2"].at[me], target,
        )

    def when_owner(index, act):
        if owners == n:
            act()
        else:
            pl.when(index < owners)(act)

    def send_states(which):
        def one(k):
            when_owner(around(k), lambda: state_copy(which, k).start())

        repeat(1, n, one)

        def own():
            r[which + "_got"][me] = r[which + "_own"][rows_of(me), :]

        when_owner(me, own)

    def scan_states(which, reverse):
        def act():
            def arrive(k):
                source = around(k)
                remote(
                    r[which + "_own"].at[rows_of(0)], r[which + "_got"].at[source],
                    r[which + "_s1"].at[0], r[which + "_r1"].at[source], me,
                ).wait_recv()

            repeat(1, n, arrive)

            def lap(k, acc):
                at = n - 1 - k if reverse else k
                r[which + "_sums"][at] = acc.astype(BF16)
                return acc + r[which + "_got"][at].astype(F32)

            acc = jnp.zeros((piece, HD), F32)
            if n <= 16:
                for k in range(n):
                    acc = lap(k, acc)
            else:
                lax.fori_loop(0, n, lap, acc)
            repeat(1, n, lambda k: total_copy(which, k).start())
            r[which + "_all"][rows_of(me), :] = r[which + "_sums"][me]

        when_owner(me, act)

    def take_totals(which):
        def one(k):
            source = around(k)

            def act():
                remote(
                    r[which + "_sums"].at[0], r[which + "_all"].at[rows_of(source)],
                    r[which + "_s2"].at[0], r[which + "_r2"].at[source], me,
                ).wait_recv()

            when_owner(source, act)

        repeat(1, n, one)

    def finish_states(which):
        def one(k):
            when_owner(around(k), lambda: state_copy(which, k).wait_send())

        repeat(1, n, one)
        when_owner(me, lambda: repeat(1, n, lambda k: total_copy(which, k).wait_send()))

    def slot(d):
        return pl.ds(d * rows, rows)

    def halo(name, source, d):
        forward = name in ("kx", "vx")
        return remote(
            r[source], r[name].at[slot(d)],
            r[name + "_s"].at[d], r[name + "_r"].at[d], me + d if forward else me - d,
        )

    def halo_sends(d, act):
        @pl.when(me + d < n)
        def _():
            act(halo("kx", "wk", d))
            act(halo("vx", "wv", d))

        @pl.when(me - d >= 0)
        def _():
            act(halo("qx", "wq", d))
            act(halo("gx", "go", d))

    def stat_copy(d):
        return remote(
            r["stat_own"], r["stat"].at[d], r["stat_s"].at[d], r["stat_r"].at[d], me - d
        )

    def norm_copy(k):
        target = lax.rem(hme + k, hn)
        return remote(
            r["norm_own"], r["norm"].at[hme], r["norm_s"].at[target], r["norm_r"].at[hme],
            target, "head",
        )

    row_id = lax.broadcasted_iota(jnp.int32, (rows, rows), 0)
    col_id = lax.broadcasted_iota(jnp.int32, (rows, rows), 1)
    causal = row_id >= col_id
    lane = lax.broadcasted_iota(jnp.int32, (rows, HD), 1)

    for h in range(heads):
        r["ks_own"][col[h], :] = dot_tn(r["lk"][:, col[h]], r["lv"][:, col[h]]).astype(BF16)

    pl.semaphore_wait(barrier, n - 1 + hn - 1)
    send_states("ks")
    for d in range(1, span + 1):
        halo_sends(d, lambda copy: copy.start())

    zero_block = jnp.zeros((rows, cols), BF16)
    r["kx"][slot(0), :] = r["wk"][...]
    r["vx"][slot(0), :] = r["wv"][...]
    r["qx"][slot(0), :] = r["wq"][...]
    r["gx"][slot(0), :] = r["go"][...]
    for h in range(heads):
        scores = jnp.where(causal, dot_nt(r["lq"][:, col[h]], r["lk"][:, col[h]]), 0.0)
        low = scores.astype(BF16)
        r["lin_scores"][h] = low
        r["lin_out"][:, col[h]] = dot_nn(low, r["lv"][:, col[h]])

    scan_states("ks", False)

    def query_scores(d):
        at = slot(d)
        for h in range(heads):
            s = dot_nt(r["wq"][:, col[h]], r["kx"][at, col[h]]) * scale
            if d == 0:
                s = jnp.where(causal, s, NEG)
            elif d == span:
                s = jnp.where(row_id < col_id, s, NEG)
            r["s"][h, :, at] = s
            r["dp"][h, :, at] = dot_nt(r["go"][:, col[h]], r["vx"][at, col[h]])

    def query_block(d):
        @pl.when(me - d >= 0)
        def _():
            halo("kx", "wk", d).wait_recv()
            halo("vx", "wv", d).wait_recv()
            query_scores(d)

        @pl.when(me - d < 0)
        def _():
            r["kx"][slot(d), :] = zero_block
            r["vx"][slot(d), :] = zero_block
            for h in range(heads):
                r["s"][h, :, slot(d)] = jnp.full((rows, rows), NEG, F32)
                r["dp"][h, :, slot(d)] = jnp.zeros((rows, rows), F32)

    query_scores(0)

    take_totals("ks")
    square = jnp.zeros((rows, 1), F32)
    cross = jnp.zeros((rows, 1), F32)
    for h in range(heads):
        out = r["lin_out"][:, col[h]] + dot_nn(r["lq"][:, col[h]], r["ks_all"][col[h], :])
        r["lin_out"][:, col[h]] = out
        square += jnp.sum(out * out, axis=1, keepdims=True)
        cross += jnp.sum(out * r["go"][:, col[h]].astype(F32), axis=1, keepdims=True)
    norm_tile = jnp.where(lane == 0, square, jnp.where(lane == 1, cross, 0.0))
    norm_rows = norm_tile.T[:8]
    r["norm_own"][...] = norm_rows
    for k in range(1, hn):
        norm_copy(k).start()

    query_block(1)

    for k in range(1, hn):
        source = lax.rem(hme + k, hn)
        remote(
            r["norm_own"], r["norm"].at[source], r["norm_s"].at[0], r["norm_r"].at[source],
            hme, "head",
        ).wait_recv()
    r["norm"][hme] = norm_rows
    norm_sum = r["norm"][0]
    for k in range(1, hn):
        norm_sum = norm_sum + r["norm"][k]
    inv_row = lax.rsqrt(norm_sum[0:1] / features + NORM_EPS)
    pull_row = inv_row * inv_row * inv_row * norm_sum[1:2] / features
    inv = jnp.broadcast_to(inv_row, (HD, rows)).T
    pull = jnp.broadcast_to(pull_row, (HD, rows)).T
    for h in range(heads):
        out = r["lin_out"][:, col[h]]
        dout = (inv * r["go"][:, col[h]].astype(F32) - out * pull).astype(BF16)
        r["lin_dout"][:, col[h]] = dout
        r["lin_out"][:, col[h]] = out * inv
        r["qs_own"][col[h], :] = dot_tn(r["lq"][:, col[h]], dout).astype(BF16)
    send_states("qs")

    for h in range(heads):
        dout = r["lin_dout"][:, col[h]]
        back = jnp.where(causal, dot_nt(dout, r["lv"][:, col[h]]), 0.0).astype(BF16)
        grad = dot_nn(back, r["lk"][:, col[h]]) + dot_nt(dout, r["ks_all"][col[h], :])
        r["glq"][:, col[h]] = grad.astype(BF16)
        r["grad_k"][:, col[h]] = dot_tn(back, r["lq"][:, col[h]])
        r["grad_v"][:, col[h]] = dot_tn(r["lin_scores"][h], dout)

    scan_states("qs", True)

    for d in range(2, span + 1):
        query_block(d)

    stat_tile = jnp.zeros((rows, HD), F32)
    kept = []
    for h in range(heads):
        s = r["s"][h]
        top = jnp.max(s, axis=1, keepdims=True)
        e = jnp.exp(s - top)
        total = jnp.sum(e, axis=1, keepdims=True)
        probs = e * (1.0 / total)
        dp = r["dp"][h]
        dots = jnp.sum(probs * dp, axis=1, keepdims=True)
        stat_tile = jnp.where(lane == 2 * h, top + jnp.log(total), stat_tile)
        stat_tile = jnp.where(lane == 2 * h + 1, dots, stat_tile)
        r["s"][h] = probs
        kept.append(dots)
    stat_rows = stat_tile.T[: r["stat_own"].shape[0]]
    r["stat_own"][...] = stat_rows
    for d in range(1, span + 1):
        pl.when(me - d >= 0)(lambda d=d: stat_copy(d).start())
    r["stat"][0] = stat_rows
    for h in range(heads):
        probs = r["s"][h]
        ds = (probs * (r["dp"][h] - kept[h]) * scale).astype(BF16)
        mixed = r["lin_out"][:, col[h]] + dot_nn(probs.astype(BF16), r["vx"][:, col[h]])
        r["mixed"][:, col[h]] = mixed.astype(BF16)
        r["gwq"][:, col[h]] = dot_nn(ds, r["kx"][:, col[h]]).astype(BF16)

    take_totals("qs")
    for h in range(heads):
        after = r["qs_all"][col[h], :]
        grad_k = r["grad_k"][:, col[h]] + dot_nt(r["lv"][:, col[h]], after)
        grad_v = r["grad_v"][:, col[h]] + dot_nn(r["lk"][:, col[h]], after)
        r["glk"][:, col[h]] = grad_k.astype(BF16)
        r["glv"][:, col[h]] = grad_v.astype(BF16)

    for d in range(1, span + 1):

        @pl.when(me + d < n)
        def _():
            halo("qx", "wq", d).wait_recv()
            halo("gx", "go", d).wait_recv()

        @pl.when(me + d >= n)
        def _():
            r["qx"][slot(d), :] = zero_block
            r["gx"][slot(d), :] = zero_block

    for h in range(heads):
        r["s"][h] = dot_nt(r["wk"][:, col[h]], r["qx"][:, col[h]]) * scale
        r["dp"][h] = dot_nt(r["wv"][:, col[h]], r["gx"][:, col[h]])

    for d in range(1, span + 1):

        @pl.when(me + d < n)
        def _():
            stat_copy(d).wait_recv()

        @pl.when(me + d >= n)
        def _():
            r["stat"][d] = jnp.full(stat_rows.shape, -NEG, F32)

    for h in range(heads):
        for d in range(span + 1):
            at = slot(d)
            s = r["s"][h, :, at] - r["stat"][d, 2 * h : 2 * h + 1, :]
            if d == 0:
                s = jnp.where(col_id >= row_id, s, NEG)
            elif d == span:
                s = jnp.where(col_id < row_id, s, NEG)
            probs = jnp.exp(s)
            ds = probs * (r["dp"][h, :, at] - r["stat"][d, 2 * h + 1 : 2 * h + 2, :]) * scale
            r["p_low"][h, :, at] = probs.astype(BF16)
            r["ds_low"][h, :, at] = ds.astype(BF16)
        r["gwk"][:, col[h]] = dot_nn(r["ds_low"][h], r["qx"][:, col[h]]).astype(BF16)
        r["gwv"][:, col[h]] = dot_nn(r["p_low"][h], r["gx"][:, col[h]]).astype(BF16)

    finish_states("ks")
    finish_states("qs")
    for d in range(1, span + 1):
        halo_sends(d, lambda copy: copy.wait_send())
        pl.when(me - d >= 0)(lambda d=d: stat_copy(d).wait_send())
    for k in range(1, hn):
        norm_copy(k).wait_send()


def shards(n, hn, *arrays):
    rows, cols = arrays[0].shape
    heads = cols // HD
    span = WIN // rows
    owners = owner_count(n, heads * HD)
    piece = heads * HD // owners
    ext = (span + 1) * rows
    stat_rows = -(-2 * heads // 8) * 8
    dma = pltpu.SemaphoreType.DMA
    scratch = {}
    for which in ("ks", "qs"):
        scratch[which + "_own"] = pltpu.VMEM((heads * HD, HD), BF16)
        scratch[which + "_got"] = pltpu.VMEM((n, piece, HD), BF16)
        scratch[which + "_sums"] = pltpu.VMEM((n, piece, HD), BF16)
        scratch[which + "_all"] = pltpu.VMEM((heads * HD, HD), BF16)
        for sem in ("_s1", "_r1", "_s2", "_r2"):
            scratch[which + sem] = dma((n,))
    for name in ("kx", "vx", "qx", "gx"):
        scratch[name] = pltpu.VMEM((ext, cols), BF16)
        scratch[name + "_s"] = dma((span + 1,))
        scratch[name + "_r"] = dma((span + 1,))
    scratch["stat_own"] = pltpu.VMEM((stat_rows, rows), F32)
    scratch["stat"] = pltpu.VMEM((span + 1, stat_rows, rows), F32)
    scratch["stat_s"] = dma((span + 1,))
    scratch["stat_r"] = dma((span + 1,))
    scratch["norm_own"] = pltpu.VMEM((8, rows), F32)
    scratch["norm"] = pltpu.VMEM((hn, 8, rows), F32)
    scratch["norm_s"] = dma((hn,))
    scratch["norm_r"] = dma((hn,))
    scratch["lin_scores"] = pltpu.VMEM((heads, rows, rows), BF16)
    scratch["lin_out"] = pltpu.VMEM((rows, cols), F32)
    scratch["lin_dout"] = pltpu.VMEM((rows, cols), BF16)
    scratch["grad_k"] = pltpu.VMEM((rows, cols), F32)
    scratch["grad_v"] = pltpu.VMEM((rows, cols), F32)
    scratch["s"] = pltpu.VMEM((heads, rows, ext), F32)
    scratch["dp"] = pltpu.VMEM((heads, rows, ext), F32)
    scratch["p_low"] = pltpu.VMEM((heads, rows, ext), BF16)
    scratch["ds_low"] = pltpu.VMEM((heads, rows, ext), BF16)
    names = IN_NAMES + OUT_NAMES + tuple(scratch)
    flops = 2 * rows * HD * heads * (8 * ext + 14 * HD)
    vmem = pl.BlockSpec(memory_space=pltpu.VMEM)
    outs = pl.pallas_call(
        partial(kernel, n, hn, owners, span, names),
        out_shape=[jax.ShapeDtypeStruct((rows, cols), BF16)] * len(OUT_NAMES),
        in_specs=[vmem] * len(IN_NAMES),
        out_specs=[vmem] * len(OUT_NAMES),
        scratch_shapes=list(scratch.values()),
        compiler_params=pltpu.CompilerParams(
            collective_id=0, has_side_effects=True, vmem_limit_bytes=40 * 2**20
        ),
        cost_estimate=pl.CostEstimate(
            flops=flops, bytes_accessed=14 * rows * cols * 2, transcendentals=2 * heads * rows * ext
        ),
    )(*arrays)
    return tuple(outs)


def solution(mesh):
    split = P("ctx", "head")
    return jax.shard_map(
        partial(shards, mesh.shape["ctx"], mesh.shape["head"]),
        mesh=mesh,
        in_specs=(split,) * len(IN_NAMES),
        out_specs=(split,) * len(OUT_NAMES),
        check_vma=False,
    )
```

```python
from functools import partial
import math

import jax
import jax.numpy as jnp
from jax import lax
from jax.experimental import pallas as pl
from jax.experimental.pallas import tpu as pltpu
from jax.sharding import PartitionSpec as P

HD = 128
WIN = 512
NORM_EPS = 1e-05
NEG = -1e30
MESH = pl.DeviceIdType.MESH
F32 = jnp.float32
BF16 = jnp.bfloat16

IN_NAMES = ("lq", "lk", "lv", "wq", "wk", "wv", "go")
FETCH_ORDER = (1, 2, 0, 4, 3, 5, 6)
BLOCK_OF = {"kx": "wk", "vx": "wv", "qx": "wq", "gx": "go"}
OUT_NAMES = ("mixed", "glq", "glk", "glv", "gwq", "gwk", "gwv")


def dot_nn(a, b):
    return lax.dot_general(a, b, (((1,), (0,)), ((), ())), preferred_element_type=F32)


def dot_nt(a, b):
    return lax.dot_general(a, b, (((1,), (1,)), ((), ())), preferred_element_type=F32)


def dot_tn(a, b):
    return lax.dot_general(a, b, (((0,), (0,)), ((), ())), preferred_element_type=F32)


def repeat(low, high, step):
    if high - low <= 16:
        for k in range(low, high):
            step(k)
    else:

        def body(k, carry):
            step(k)
            return carry

        lax.fori_loop(low, high, body, 0)


def owner_count(n, state_rows):
    owners = 1
    while owners * 2 <= n and state_rows % (owners * 2 * 16) == 0:
        owners *= 2
    return owners


def kernel(n, hn, owners, span, names, *refs):
    r = dict(zip(names, refs))
    rows, cols = r["lq_in"].shape
    heads = cols // HD
    me = lax.axis_index("ctx")
    hme = lax.axis_index("head")
    piece = heads * HD // owners
    scale = 1.0 / math.sqrt(HD)
    features = cols * hn
    col = [slice(h * HD, (h + 1) * HD) for h in range(heads)]

    def around(k):
        return lax.rem(me + k, n)

    def remote(src, dst, send, recv, target, axis="ctx"):
        return pltpu.make_async_remote_copy(
            src_ref=src, dst_ref=dst, send_sem=send, recv_sem=recv,
            device_id={axis: target}, device_id_type=MESH,
        )

    barrier = pltpu.get_barrier_semaphore()

    def greet(k):
        pl.semaphore_signal(barrier, inc=1, device_id={"ctx": around(k)}, device_id_type=MESH)

    repeat(1, n, greet)
    for k in range(1, hn):
        pl.semaphore_signal(
            barrier, inc=1, device_id={"head": lax.rem(hme + k, hn)}, device_id_type=MESH
        )

    def rows_of(owner):
        return pl.ds(pl.multiple_of(owner * piece, piece), piece)

    def state_copy(which, k):
        target = around(k)
        return remote(
            r[which + "_own"].at[rows_of(target)], r[which + "_got"].at[me],
            r[which + "_s1"].at[target], r[which + "_r1"].at[me], target,
        )

    def total_copy(which, k):
        target = around(k)
        return remote(
            r[which + "_sums"].at[target], r[which + "_all"].at[rows_of(me)],
            r[which + "_s2"].at[target], r[which + "_r2"].at[me], target,
        )

    def when_owner(index, act):
        if owners == n:
            act()
        else:
            pl.when(index < owners)(act)

    def send_states(which):
        def one(k):
            when_owner(around(k), lambda: state_copy(which, k).start())

        repeat(1, n, one)

        def own():
            r[which + "_got"][me] = r[which + "_own"][rows_of(me), :]

        when_owner(me, own)

    def scan_states(which, reverse):
        def act():
            def arrive(k):
                source = around(k)
                remote(
                    r[which + "_own"].at[rows_of(0)], r[which + "_got"].at[source],
                    r[which + "_s1"].at[0], r[which + "_r1"].at[source], me,
                ).wait_recv()

            repeat(1, n, arrive)

            def lap(k, acc):
                at = n - 1 - k if reverse else k
                r[which + "_sums"][at] = acc.astype(BF16)
                return acc + r[which + "_got"][at].astype(F32)

            acc = jnp.zeros((piece, HD), F32)
            if n <= 16:
                for k in range(n):
                    acc = lap(k, acc)
            else:
                lax.fori_loop(0, n, lap, acc)
            repeat(1, n, lambda k: total_copy(which, k).start())
            r[which + "_all"][rows_of(me), :] = r[which + "_sums"][me]

        when_owner(me, act)

    def take_totals(which):
        def one(k):
            source = around(k)

            def act():
                remote(
                    r[which + "_sums"].at[0], r[which + "_all"].at[rows_of(source)],
                    r[which + "_s2"].at[0], r[which + "_r2"].at[source], me,
                ).wait_recv()

            when_owner(source, act)

        repeat(1, n, one)

    def finish_states(which):
        def one(k):
            when_owner(around(k), lambda: state_copy(which, k).wait_send())

        repeat(1, n, one)
        when_owner(me, lambda: repeat(1, n, lambda k: total_copy(which, k).wait_send()))

    def slot(d):
        return pl.ds(d * rows, rows)

    side = {"kx": 1, "vx": 1, "qx": -1, "gx": -1}
    odd = lax.rem(me, 2) == 1
    leads = {1: jnp.logical_not(odd), -1: odd}

    def there(index):
        return jnp.logical_and(index >= 0, index < n)

    hops = {"own": (0, 2, 2), "pair": (0, 1, 1), "far": (2, 2, 4), "back": (2, -1, 1), "near": (1, 2, 3)}
    hop_ids = {hop: i for i, hop in enumerate(hops)}

    def hop_copy(name, hop):
        sent, offset, filled = hops[hop]
        source = r[BLOCK_OF[name] + "_in"] if sent == 0 else r[name].at[slot(sent)]
        return remote(
            source, r[name].at[slot(filled)], r[name + "_s"].at[hop_ids[hop]],
            r[name + "_r"].at[filled], me + side[name] * offset,
        )

    def hop_taken(name, hop):
        sent, offset, _ = hops[hop]
        way = side[name]
        taken = there(me + way * offset)
        if sent:
            taken = jnp.logical_and(taken, there(me - way * sent))
        if hop == "pair":
            taken = jnp.logical_and(taken, leads[way])
        if hop == "back":
            taken = jnp.logical_and(taken, jnp.logical_not(leads[way]))
        return taken

    def hop_all(names, hop, act):
        @pl.when(hop_taken(names[0], hop))
        def _():
            for name in names:
                act(hop_copy(name, hop))

    def arrived(names, d):
        @pl.when(there(me - side[names[0]] * d))
        def _():
            for name in names:
                remote(
                    r[BLOCK_OF[name] + "_in"], r[name].at[slot(d)], r[name + "_s"].at[0],
                    r[name + "_r"].at[d], me,
                ).wait_recv()

    def start(copy):
        copy.start()

    keys_side, query_side = ("kx", "vx"), ("qx", "gx")

    def fetch(i):
        name = IN_NAMES[i]
        slot_of = {"wk": "kx", "wv": "vx", "wq": "qx", "go": "gx"}
        target = r[slot_of[name]].at[slot(0)] if name in slot_of else r[name]
        return pltpu.make_async_copy(r[name + "_in"], target, r["fetch"].at[i])

    def stat_copy(d):
        return remote(
            r["stat_own"], r["stat"].at[d], r["stat_s"].at[d], r["stat_r"].at[d], me - d
        )

    def norm_copy(k):
        target = lax.rem(hme + k, hn)
        return remote(
            r["norm_own"], r["norm"].at[hme], r["norm_s"].at[target], r["norm_r"].at[hme],
            target, "head",
        )

    row_id = lax.broadcasted_iota(jnp.int32, (rows, rows), 0)
    col_id = lax.broadcasted_iota(jnp.int32, (rows, rows), 1)
    causal = row_id >= col_id
    lane = lax.broadcasted_iota(jnp.int32, (rows, HD), 1)

    for i in FETCH_ORDER:
        fetch(i).start()
    fetch(1).wait()
    fetch(2).wait()
    for h in range(heads):
        r["ks_own"][col[h], :] = dot_tn(r["lk"][:, col[h]], r["lv"][:, col[h]]).astype(BF16)

    pl.semaphore_wait(barrier, n - 1 + hn - 1)
    send_states("ks")
    for names in (keys_side, query_side):
        hop_all(names, "own", start)
        hop_all(names, "pair", start)

    zero_block = jnp.zeros((rows, cols), BF16)
    for i in FETCH_ORDER[2:]:
        fetch(i).wait()
    for h in range(heads):
        scores = jnp.where(causal, dot_nt(r["lq"][:, col[h]], r["lk"][:, col[h]]), 0.0)
        low = scores.astype(BF16)
        r["lin_scores"][h] = low
        r["lin_out"][:, col[h]] = dot_nn(low, r["lv"][:, col[h]])

    scan_states("ks", False)

    def query_scores(d):
        at = slot(d)
        for h in range(heads):
            s = dot_nt(r["qx"][slot(0), col[h]], r["kx"][at, col[h]]) * scale
            if d == 0:
                s = jnp.where(causal, s, NEG)
            elif d == span:
                s = jnp.where(row_id < col_id, s, NEG)
            r["s"][h, :, at] = s
            r["dp"][h, :, at] = dot_nt(r["gx"][slot(0), col[h]], r["vx"][at, col[h]])

    def query_block(d):
        @pl.when(me - d >= 0)
        def _():
            query_scores(d)

        @pl.when(me - d < 0)
        def _():
            r["kx"][slot(d), :] = zero_block
            r["vx"][slot(d), :] = zero_block
            for h in range(heads):
                r["s"][h, :, slot(d)] = jnp.full((rows, rows), NEG, F32)
                r["dp"][h, :, slot(d)] = jnp.zeros((rows, rows), F32)

    query_scores(0)

    take_totals("ks")
    square = jnp.zeros((rows, 1), F32)
    cross = jnp.zeros((rows, 1), F32)
    for h in range(heads):
        out = r["lin_out"][:, col[h]] + dot_nn(r["lq"][:, col[h]], r["ks_all"][col[h], :])
        r["lin_out"][:, col[h]] = out
        square += jnp.sum(out * out, axis=1, keepdims=True)
        cross += jnp.sum(out * r["gx"][slot(0), col[h]].astype(F32), axis=1, keepdims=True)
    norm_tile = jnp.where(lane == 0, square, jnp.where(lane == 1, cross, 0.0))
    norm_rows = norm_tile.T[:8]
    r["norm_own"][...] = norm_rows
    for k in range(1, hn):
        norm_copy(k).start()

    for names in (keys_side, query_side):
        arrived(names, 2)
        hop_all(names, "far", start)
        hop_all(names, "back", start)

    for k in range(1, hn):
        source = lax.rem(hme + k, hn)
        remote(
            r["norm_own"], r["norm"].at[source], r["norm_s"].at[0], r["norm_r"].at[source],
            hme, "head",
        ).wait_recv()
    r["norm"][hme] = norm_rows
    norm_sum = r["norm"][0]
    for k in range(1, hn):
        norm_sum = norm_sum + r["norm"][k]
    inv_row = lax.rsqrt(norm_sum[0:1] / features + NORM_EPS)
    pull_row = inv_row * inv_row * inv_row * norm_sum[1:2] / features
    inv = jnp.broadcast_to(inv_row, (HD, rows)).T
    pull = jnp.broadcast_to(pull_row, (HD, rows)).T
    for h in range(heads):
        out = r["lin_out"][:, col[h]]
        dout = (inv * r["gx"][slot(0), col[h]].astype(F32) - out * pull).astype(BF16)
        r["lin_dout"][:, col[h]] = dout
        r["lin_out"][:, col[h]] = out * inv
        r["qs_own"][col[h], :] = dot_tn(r["lq"][:, col[h]], dout).astype(BF16)
    send_states("qs")

    for names in (keys_side, query_side):
        arrived(names, 1)
        hop_all(names, "near", start)
    query_block(2)
    query_block(1)

    for h in range(heads):
        dout = r["lin_dout"][:, col[h]]
        back = jnp.where(causal, dot_nt(dout, r["lv"][:, col[h]]), 0.0).astype(BF16)
        grad = dot_nn(back, r["lk"][:, col[h]]) + dot_nt(dout, r["ks_all"][col[h], :])
        r["glq"][:, col[h]] = grad.astype(BF16)
        r["grad_k"][:, col[h]] = dot_tn(back, r["lq"][:, col[h]])
        r["grad_v"][:, col[h]] = dot_tn(r["lin_scores"][h], dout)

    scan_states("qs", True)

    for d in (3, 4):
        arrived(keys_side, d)
        query_block(d)

    stat_tile = jnp.zeros((rows, HD), F32)
    kept = []
    for h in range(heads):
        s = r["s"][h]
        top = jnp.max(s, axis=1, keepdims=True)
        e = jnp.exp(s - top)
        total = jnp.sum(e, axis=1, keepdims=True)
        probs = e * (1.0 / total)
        dp = r["dp"][h]
        dots = jnp.sum(probs * dp, axis=1, keepdims=True)
        stat_tile = jnp.where(lane == 2 * h, top + jnp.log(total), stat_tile)
        stat_tile = jnp.where(lane == 2 * h + 1, dots, stat_tile)
        r["s"][h] = probs
        kept.append(dots)
    stat_rows = stat_tile.T[: r["stat_own"].shape[0]]
    r["stat_own"][...] = stat_rows
    for d in range(1, span + 1):
        pl.when(me - d >= 0)(lambda d=d: stat_copy(d).start())
    r["stat"][0] = stat_rows
    for h in range(heads):
        probs = r["s"][h]
        ds = (probs * (r["dp"][h] - kept[h]) * scale).astype(BF16)
        mixed = r["lin_out"][:, col[h]] + dot_nn(probs.astype(BF16), r["vx"][:, col[h]])
        r["mixed"][:, col[h]] = mixed.astype(BF16)
        r["gwq"][:, col[h]] = dot_nn(ds, r["kx"][:, col[h]]).astype(BF16)

    take_totals("qs")
    for h in range(heads):
        after = r["qs_all"][col[h], :]
        grad_k = r["grad_k"][:, col[h]] + dot_nt(r["lv"][:, col[h]], after)
        grad_v = r["grad_v"][:, col[h]] + dot_nn(r["lk"][:, col[h]], after)
        r["glk"][:, col[h]] = grad_k.astype(BF16)
        r["glv"][:, col[h]] = grad_v.astype(BF16)

    for d in range(1, span + 1):
        if d > 2:
            arrived(query_side, d)

        @pl.when(me + d >= n)
        def _():
            r["qx"][slot(d), :] = zero_block
            r["gx"][slot(d), :] = zero_block

    for h in range(heads):
        r["s"][h] = dot_nt(r["kx"][slot(0), col[h]], r["qx"][:, col[h]]) * scale
        r["dp"][h] = dot_nt(r["vx"][slot(0), col[h]], r["gx"][:, col[h]])

    for d in range(1, span + 1):

        @pl.when(me + d < n)
        def _():
            stat_copy(d).wait_recv()

        @pl.when(me + d >= n)
        def _():
            r["stat"][d] = jnp.full(stat_rows.shape, -NEG, F32)

    for h in range(heads):
        for d in range(span + 1):
            at = slot(d)
            s = r["s"][h, :, at] - r["stat"][d, 2 * h : 2 * h + 1, :]
            if d == 0:
                s = jnp.where(col_id >= row_id, s, NEG)
            elif d == span:
                s = jnp.where(col_id < row_id, s, NEG)
            probs = jnp.exp(s)
            ds = probs * (r["dp"][h, :, at] - r["stat"][d, 2 * h + 1 : 2 * h + 2, :]) * scale
            r["p_low"][h, :, at] = probs.astype(BF16)
            r["ds_low"][h, :, at] = ds.astype(BF16)
        r["gwk"][:, col[h]] = dot_nn(r["ds_low"][h], r["qx"][:, col[h]]).astype(BF16)
        r["gwv"][:, col[h]] = dot_nn(r["p_low"][h], r["gx"][:, col[h]]).astype(BF16)

    finish_states("ks")
    finish_states("qs")
    for names in (keys_side, query_side):
        for hop in hops:
            hop_all(names, hop, lambda copy: copy.wait_send())
    for d in range(1, span + 1):
        pl.when(me - d >= 0)(lambda d=d: stat_copy(d).wait_send())
    for k in range(1, hn):
        norm_copy(k).wait_send()


def write_all(*refs):
    count = len(OUT_NAMES)
    copies = [
        pltpu.make_async_copy(refs[i], refs[count + i], refs[2 * count].at[i])
        for i in range(count)
    ]
    for copy in copies:
        copy.start()
    for copy in copies:
        copy.wait()


def shards(n, hn, *arrays):
    rows, cols = arrays[0].shape
    heads = cols // HD
    span = WIN // rows
    assert span == 4 and WIN % rows == 0 and n % 2 == 0
    owners = owner_count(n, heads * HD)
    piece = heads * HD // owners
    ext = (span + 1) * rows
    stat_rows = -(-2 * heads // 8) * 8
    dma = pltpu.SemaphoreType.DMA
    scratch = {}
    for which in ("ks", "qs"):
        scratch[which + "_own"] = pltpu.VMEM((heads * HD, HD), BF16)
        scratch[which + "_got"] = pltpu.VMEM((n, piece, HD), BF16)
        scratch[which + "_sums"] = pltpu.VMEM((n, piece, HD), BF16)
        scratch[which + "_all"] = pltpu.VMEM((heads * HD, HD), BF16)
        for sem in ("_s1", "_r1", "_s2", "_r2"):
            scratch[which + sem] = dma((n,))
    for name in ("kx", "vx", "qx", "gx"):
        scratch[name] = pltpu.VMEM((ext, cols), BF16)
        scratch[name + "_s"] = dma((5,))
        scratch[name + "_r"] = dma((span + 1,))
    for name in ("lq", "lk", "lv"):
        scratch[name] = pltpu.VMEM((rows, cols), BF16)
    scratch["fetch"] = dma((len(IN_NAMES),))
    scratch["stat_own"] = pltpu.VMEM((stat_rows, rows), F32)
    scratch["stat"] = pltpu.VMEM((span + 1, stat_rows, rows), F32)
    scratch["stat_s"] = dma((span + 1,))
    scratch["stat_r"] = dma((span + 1,))
    scratch["norm_own"] = pltpu.VMEM((8, rows), F32)
    scratch["norm"] = pltpu.VMEM((hn, 8, rows), F32)
    scratch["norm_s"] = dma((hn,))
    scratch["norm_r"] = dma((hn,))
    scratch["lin_scores"] = pltpu.VMEM((heads, rows, rows), BF16)
    scratch["lin_out"] = pltpu.VMEM((rows, cols), F32)
    scratch["lin_dout"] = pltpu.VMEM((rows, cols), BF16)
    scratch["grad_k"] = pltpu.VMEM((rows, cols), F32)
    scratch["grad_v"] = pltpu.VMEM((rows, cols), F32)
    scratch["s"] = pltpu.VMEM((heads, rows, ext), F32)
    scratch["dp"] = pltpu.VMEM((heads, rows, ext), F32)
    scratch["p_low"] = pltpu.VMEM((heads, rows, ext), BF16)
    scratch["ds_low"] = pltpu.VMEM((heads, rows, ext), BF16)
    names = tuple(name + "_in" for name in IN_NAMES) + OUT_NAMES + tuple(scratch)
    flops = 2 * rows * HD * heads * (8 * ext + 14 * HD)
    vmem = pl.BlockSpec(memory_space=pltpu.VMEM)
    hbm = pl.BlockSpec(memory_space=pltpu.HBM)
    outs = pl.pallas_call(
        partial(kernel, n, hn, owners, span, names),
        out_shape=[jax.ShapeDtypeStruct((rows, cols), BF16)] * len(OUT_NAMES),
        in_specs=[hbm] * len(IN_NAMES),
        out_specs=[vmem] * len(OUT_NAMES),
        scratch_shapes=list(scratch.values()),
        compiler_params=pltpu.CompilerParams(
            collective_id=0, has_side_effects=True, vmem_limit_bytes=60 * 2**20
        ),
        cost_estimate=pl.CostEstimate(
            flops=flops, bytes_accessed=14 * rows * cols * 2, transcendentals=2 * heads * rows * ext
        ),
    )(*arrays)
    shapes = [jax.ShapeDtypeStruct(out.shape, out.dtype) for out in outs]
    return tuple(
        pl.pallas_call(
            write_all,
            out_shape=shapes,
            in_specs=[hbm] * len(OUT_NAMES),
            out_specs=[hbm] * len(OUT_NAMES),
            scratch_shapes=[dma((len(OUT_NAMES),))],
            compiler_params=pltpu.CompilerParams(vmem_limit_bytes=60 * 2**20),
        )(*outs)
    )


def solution(mesh):
    split = P("ctx", "head")
    return jax.shard_map(
        partial(shards, mesh.shape["ctx"], mesh.shape["head"]),
        mesh=mesh,
        in_specs=(split,) * len(IN_NAMES),
        out_specs=(split,) * len(OUT_NAMES),
        check_vma=False,
    )
```

```python
from functools import partial
import math

import jax
import jax.numpy as jnp
from jax import lax
from jax.experimental import pallas as pl
from jax.experimental.pallas import tpu as pltpu
from jax.sharding import PartitionSpec as P

HD = 128
WIN = 512
NORM_EPS = 1e-05
NEG = -1e30
MESH = pl.DeviceIdType.MESH
F32 = jnp.float32
BF16 = jnp.bfloat16

IN_NAMES = ("lq", "lk", "lv", "wq", "wk", "wv", "go")
FETCH_ORDER = (1, 2, 0, 4, 3, 5, 6)
BLOCK_OF = {"kx": "wk", "vx": "wv", "qx": "wq", "gx": "go"}
OUT_NAMES = ("mixed", "glq", "glk", "glv", "gwq", "gwk", "gwv")


def dot_nn(a, b):
    return lax.dot_general(a, b, (((1,), (0,)), ((), ())), preferred_element_type=F32)


def dot_nt(a, b):
    return lax.dot_general(a, b, (((1,), (1,)), ((), ())), preferred_element_type=F32)


def dot_tn(a, b):
    return lax.dot_general(a, b, (((0,), (0,)), ((), ())), preferred_element_type=F32)


def repeat(low, high, step):
    if high - low <= 16:
        for k in range(low, high):
            step(k)
    else:

        def body(k, carry):
            step(k)
            return carry

        lax.fori_loop(low, high, body, 0)


def owner_count(n, state_rows):
    owners = 1
    while owners * 2 <= n and state_rows % (owners * 2 * 16) == 0:
        owners *= 2
    return owners


def kernel(n, hn, owners, span, names, *refs):
    r = dict(zip(names, refs))
    rows, cols = r["lq_in"].shape
    heads = cols // HD
    me = lax.axis_index("ctx")
    hme = lax.axis_index("head")
    piece = heads * HD // owners
    scale = 1.0 / math.sqrt(HD)
    features = cols * hn
    col = [slice(h * HD, (h + 1) * HD) for h in range(heads)]

    def around(k):
        return lax.rem(me + k, n)

    def remote(src, dst, send, recv, target, axis="ctx"):
        return pltpu.make_async_remote_copy(
            src_ref=src, dst_ref=dst, send_sem=send, recv_sem=recv,
            device_id={axis: target}, device_id_type=MESH,
        )

    barrier = pltpu.get_barrier_semaphore()

    def greet(k):
        pl.semaphore_signal(barrier, inc=1, device_id={"ctx": around(k)}, device_id_type=MESH)

    repeat(1, n, greet)
    for k in range(1, hn):
        pl.semaphore_signal(
            barrier, inc=1, device_id={"head": lax.rem(hme + k, hn)}, device_id_type=MESH
        )

    def rows_of(owner):
        return pl.ds(pl.multiple_of(owner * piece, piece), piece)

    def state_copy(which, k):
        target = around(k)
        return remote(
            r[which + "_own"].at[rows_of(target)], r[which + "_got"].at[me],
            r[which + "_s1"].at[target], r[which + "_r1"].at[me], target,
        )

    def total_copy(which, k):
        target = around(k)
        return remote(
            r[which + "_sums"].at[target], r[which + "_all"].at[rows_of(me)],
            r[which + "_s2"].at[target], r[which + "_r2"].at[me], target,
        )

    def when_owner(index, act):
        if owners == n:
            act()
        else:
            pl.when(index < owners)(act)

    def send_states(which):
        def one(k):
            when_owner(around(k), lambda: state_copy(which, k).start())

        repeat(1, n, one)

        def own():
            r[which + "_got"][me] = r[which + "_own"][rows_of(me), :]

        when_owner(me, own)

    def scan_states(which, reverse):
        def act():
            def arrive(k):
                source = around(k)
                remote(
                    r[which + "_own"].at[rows_of(0)], r[which + "_got"].at[source],
                    r[which + "_s1"].at[0], r[which + "_r1"].at[source], me,
                ).wait_recv()

            repeat(1, n, arrive)

            def lap(k, acc):
                at = n - 1 - k if reverse else k
                r[which + "_sums"][at] = acc.astype(BF16)
                return acc + r[which + "_got"][at].astype(F32)

            acc = jnp.zeros((piece, HD), F32)
            if n <= 16:
                for k in range(n):
                    acc = lap(k, acc)
            else:
                lax.fori_loop(0, n, lap, acc)
            repeat(1, n, lambda k: total_copy(which, k).start())
            r[which + "_all"][rows_of(me), :] = r[which + "_sums"][me]

        when_owner(me, act)

    def take_totals(which):
        def one(k):
            source = around(k)

            def act():
                remote(
                    r[which + "_sums"].at[0], r[which + "_all"].at[rows_of(source)],
                    r[which + "_s2"].at[0], r[which + "_r2"].at[source], me,
                ).wait_recv()

            when_owner(source, act)

        repeat(1, n, one)

    def finish_states(which):
        def one(k):
            when_owner(around(k), lambda: state_copy(which, k).wait_send())

        repeat(1, n, one)
        when_owner(me, lambda: repeat(1, n, lambda k: total_copy(which, k).wait_send()))

    def slot(d):
        return pl.ds(d * rows, rows)

    side = {"kx": 1, "vx": 1, "qx": -1, "gx": -1}
    odd = lax.rem(me, 2) == 1
    leads = {1: jnp.logical_not(odd), -1: odd}

    def there(index):
        return jnp.logical_and(index >= 0, index < n)

    hops = {"own": (0, 2, 2), "pair": (0, 1, 1), "far": (2, 2, 4), "back": (2, -1, 1), "near": (1, 2, 3)}
    hop_ids = {hop: i for i, hop in enumerate(hops)}

    def hop_copy(name, hop):
        sent, offset, filled = hops[hop]
        source = r[BLOCK_OF[name] + "_in"] if sent == 0 else r[name].at[slot(sent)]
        return remote(
            source, r[name].at[slot(filled)], r[name + "_s"].at[hop_ids[hop]],
            r[name + "_r"].at[filled], me + side[name] * offset,
        )

    def hop_taken(name, hop):
        sent, offset, _ = hops[hop]
        way = side[name]
        taken = there(me + way * offset)
        if sent:
            taken = jnp.logical_and(taken, there(me - way * sent))
        if hop == "pair":
            taken = jnp.logical_and(taken, leads[way])
        if hop == "back":
            taken = jnp.logical_and(taken, jnp.logical_not(leads[way]))
        return taken

    def hop_all(names, hop, act):
        @pl.when(hop_taken(names[0], hop))
        def _():
            for name in names:
                act(hop_copy(name, hop))

    def arrived(names, d):
        @pl.when(there(me - side[names[0]] * d))
        def _():
            for name in names:
                remote(
                    r[BLOCK_OF[name] + "_in"], r[name].at[slot(d)], r[name + "_s"].at[0],
                    r[name + "_r"].at[d], me,
                ).wait_recv()

    def start(copy):
        copy.start()

    keys_side, query_side = ("kx", "vx"), ("qx", "gx")

    def fetch(i):
        name = IN_NAMES[i]
        slot_of = {"wk": "kx", "wv": "vx", "wq": "qx", "go": "gx"}
        target = r[slot_of[name]].at[slot(0)] if name in slot_of else r[name]
        return pltpu.make_async_copy(r[name + "_in"], target, r["fetch"].at[i])

    def stat_copy(d):
        return remote(
            r["stat_own"], r["stat"].at[d], r["stat_s"].at[d], r["stat_r"].at[d], me - d
        )

    def norm_copy(k):
        target = lax.rem(hme + k, hn)
        return remote(
            r["norm_own"], r["norm"].at[hme], r["norm_s"].at[target], r["norm_r"].at[hme],
            target, "head",
        )

    row_id = lax.broadcasted_iota(jnp.int32, (rows, rows), 0)
    col_id = lax.broadcasted_iota(jnp.int32, (rows, rows), 1)
    causal = row_id >= col_id
    lane = lax.broadcasted_iota(jnp.int32, (rows, HD), 1)

    for i in FETCH_ORDER:
        fetch(i).start()
    fetch(1).wait()
    fetch(2).wait()
    for h in range(heads):
        r["ks_own"][col[h], :] = dot_tn(r["lk"][:, col[h]], r["lv"][:, col[h]]).astype(BF16)

    pl.semaphore_wait(barrier, n - 1 + hn - 1)
    send_states("ks")
    for names in (keys_side, query_side):
        hop_all(names, "own", start)
        hop_all(names, "pair", start)

    zero_block = jnp.zeros((rows, cols), BF16)
    for i in FETCH_ORDER[2:]:
        fetch(i).wait()
    for h in range(heads):
        scores = jnp.where(causal, dot_nt(r["lq"][:, col[h]], r["lk"][:, col[h]]), 0.0)
        low = scores.astype(BF16)
        r["lin_scores"][h] = low
        r["lin_out"][:, col[h]] = dot_nn(low, r["lv"][:, col[h]])

    scan_states("ks", False)

    def query_scores(d):
        at = slot(d)
        for h in range(heads):
            s = dot_nt(r["qx"][slot(0), col[h]], r["kx"][at, col[h]]) * scale
            if d == 0:
                s = jnp.where(causal, s, NEG)
            elif d == span:
                s = jnp.where(row_id < col_id, s, NEG)
            r["s"][h, :, at] = s
            r["dp"][h, :, at] = dot_nt(r["gx"][slot(0), col[h]], r["vx"][at, col[h]])

    def query_block(d):
        @pl.when(me - d >= 0)
        def _():
            query_scores(d)

        @pl.when(me - d < 0)
        def _():
            r["kx"][slot(d), :] = zero_block
            r["vx"][slot(d), :] = zero_block
            for h in range(heads):
                r["s"][h, :, slot(d)] = jnp.full((rows, rows), NEG, F32)
                r["dp"][h, :, slot(d)] = jnp.zeros((rows, rows), F32)

    query_scores(0)

    take_totals("ks")
    square = jnp.zeros((rows, 1), F32)
    cross = jnp.zeros((rows, 1), F32)
    for h in range(heads):
        out = r["lin_out"][:, col[h]] + dot_nn(r["lq"][:, col[h]], r["ks_all"][col[h], :])
        r["lin_out"][:, col[h]] = out
        square += jnp.sum(out * out, axis=1, keepdims=True)
        cross += jnp.sum(out * r["gx"][slot(0), col[h]].astype(F32), axis=1, keepdims=True)
    norm_tile = jnp.where(lane == 0, square, jnp.where(lane == 1, cross, 0.0))
    norm_rows = norm_tile.T[:8]
    r["norm_own"][...] = norm_rows
    for k in range(1, hn):
        norm_copy(k).start()

    for names in (keys_side, query_side):
        arrived(names, 2)
        hop_all(names, "far", start)
        hop_all(names, "back", start)

    for k in range(1, hn):
        source = lax.rem(hme + k, hn)
        remote(
            r["norm_own"], r["norm"].at[source], r["norm_s"].at[0], r["norm_r"].at[source],
            hme, "head",
        ).wait_recv()
    r["norm"][hme] = norm_rows
    norm_sum = r["norm"][0]
    for k in range(1, hn):
        norm_sum = norm_sum + r["norm"][k]
    inv_row = lax.rsqrt(norm_sum[0:1] / features + NORM_EPS)
    pull_row = inv_row * inv_row * inv_row * norm_sum[1:2] / features
    inv = jnp.broadcast_to(inv_row, (HD, rows)).T
    pull = jnp.broadcast_to(pull_row, (HD, rows)).T
    for h in range(heads):
        out = r["lin_out"][:, col[h]]
        dout = (inv * r["gx"][slot(0), col[h]].astype(F32) - out * pull).astype(BF16)
        r["lin_dout"][:, col[h]] = dout
        r["lin_out"][:, col[h]] = out * inv
        r["qs_own"][col[h], :] = dot_tn(r["lq"][:, col[h]], dout).astype(BF16)
    send_states("qs")

    for names in (keys_side, query_side):
        arrived(names, 1)
        hop_all(names, "near", start)
    query_block(2)
    query_block(1)

    for h in range(heads):
        dout = r["lin_dout"][:, col[h]]
        back = jnp.where(causal, dot_nt(dout, r["lv"][:, col[h]]), 0.0).astype(BF16)
        grad = dot_nn(back, r["lk"][:, col[h]]) + dot_nt(dout, r["ks_all"][col[h], :])
        r["glq"][:, col[h]] = grad.astype(BF16)
        r["grad_k"][:, col[h]] = dot_tn(back, r["lq"][:, col[h]])
        r["grad_v"][:, col[h]] = dot_tn(r["lin_scores"][h], dout)

    scan_states("qs", True)

    for d in (3, 4):
        arrived(keys_side, d)
        query_block(d)

    stat_tile = jnp.zeros((rows, HD), F32)
    kept = []
    for h in range(heads):
        s = r["s"][h]
        top = jnp.max(s, axis=1, keepdims=True)
        e = jnp.exp(s - top)
        total = jnp.sum(e, axis=1, keepdims=True)
        probs = e * (1.0 / total)
        dp = r["dp"][h]
        dots = jnp.sum(probs * dp, axis=1, keepdims=True)
        stat_tile = jnp.where(lane == 2 * h, top + jnp.log(total), stat_tile)
        stat_tile = jnp.where(lane == 2 * h + 1, dots, stat_tile)
        r["s"][h] = probs
        kept.append(dots)
    stat_rows = stat_tile.T[: r["stat_own"].shape[0]]
    r["stat_own"][...] = stat_rows
    for d in range(1, span + 1):
        pl.when(me - d >= 0)(lambda d=d: stat_copy(d).start())
    r["stat"][0] = stat_rows
    for h in range(heads):
        probs = r["s"][h]
        ds = (probs * (r["dp"][h] - kept[h]) * scale).astype(BF16)
        mixed = r["lin_out"][:, col[h]] + dot_nn(probs.astype(BF16), r["vx"][:, col[h]])
        r["mixed"][:, col[h]] = mixed.astype(BF16)
        r["gwq"][:, col[h]] = dot_nn(ds, r["kx"][:, col[h]]).astype(BF16)

    take_totals("qs")
    for h in range(heads):
        after = r["qs_all"][col[h], :]
        grad_k = r["grad_k"][:, col[h]] + dot_nt(r["lv"][:, col[h]], after)
        grad_v = r["grad_v"][:, col[h]] + dot_nn(r["lk"][:, col[h]], after)
        r["glk"][:, col[h]] = grad_k.astype(BF16)
        r["glv"][:, col[h]] = grad_v.astype(BF16)

    for d in range(1, span + 1):
        if d > 2:
            arrived(query_side, d)

        @pl.when(me + d >= n)
        def _():
            r["qx"][slot(d), :] = zero_block
            r["gx"][slot(d), :] = zero_block

    for h in range(heads):
        r["s"][h] = dot_nt(r["kx"][slot(0), col[h]], r["qx"][:, col[h]]) * scale
        r["dp"][h] = dot_nt(r["vx"][slot(0), col[h]], r["gx"][:, col[h]])

    for d in range(1, span + 1):

        @pl.when(me + d < n)
        def _():
            stat_copy(d).wait_recv()

        @pl.when(me + d >= n)
        def _():
            r["stat"][d] = jnp.full(stat_rows.shape, -NEG, F32)

    for h in range(heads):
        for d in range(span + 1):
            at = slot(d)
            s = r["s"][h, :, at] - r["stat"][d, 2 * h : 2 * h + 1, :]
            if d == 0:
                s = jnp.where(col_id >= row_id, s, NEG)
            elif d == span:
                s = jnp.where(col_id < row_id, s, NEG)
            probs = jnp.exp(s)
            ds = probs * (r["dp"][h, :, at] - r["stat"][d, 2 * h + 1 : 2 * h + 2, :]) * scale
            r["p_low"][h, :, at] = probs.astype(BF16)
            r["ds_low"][h, :, at] = ds.astype(BF16)
        r["gwk"][:, col[h]] = dot_nn(r["ds_low"][h], r["qx"][:, col[h]]).astype(BF16)
        r["gwv"][:, col[h]] = dot_nn(r["p_low"][h], r["gx"][:, col[h]]).astype(BF16)

    finish_states("ks")
    finish_states("qs")
    for names in (keys_side, query_side):
        for hop in hops:
            hop_all(names, hop, lambda copy: copy.wait_send())
    for d in range(1, span + 1):
        pl.when(me - d >= 0)(lambda d=d: stat_copy(d).wait_send())
    for k in range(1, hn):
        norm_copy(k).wait_send()


def write_all(*refs):
    count = len(OUT_NAMES)
    held, sems = refs[2 * count], refs[2 * count + 1]
    ins = [pltpu.make_async_copy(refs[i], held.at[i], sems.at[i]) for i in range(count)]
    outs = [
        pltpu.make_async_copy(held.at[i], refs[count + i], sems.at[count + i])
        for i in range(count)
    ]
    for copy in ins:
        copy.start()
    for arrival, copy in zip(ins, outs):
        arrival.wait()
        copy.start()
    for copy in outs:
        copy.wait()


def shards(n, hn, *arrays):
    rows, cols = arrays[0].shape
    heads = cols // HD
    span = WIN // rows
    assert span == 4 and WIN % rows == 0 and n % 2 == 0
    owners = owner_count(n, heads * HD)
    piece = heads * HD // owners
    ext = (span + 1) * rows
    stat_rows = -(-2 * heads // 8) * 8
    dma = pltpu.SemaphoreType.DMA
    scratch = {}
    for which in ("ks", "qs"):
        scratch[which + "_own"] = pltpu.VMEM((heads * HD, HD), BF16)
        scratch[which + "_got"] = pltpu.VMEM((n, piece, HD), BF16)
        scratch[which + "_sums"] = pltpu.VMEM((n, piece, HD), BF16)
        scratch[which + "_all"] = pltpu.VMEM((heads * HD, HD), BF16)
        for sem in ("_s1", "_r1", "_s2", "_r2"):
            scratch[which + sem] = dma((n,))
    for name in ("kx", "vx", "qx", "gx"):
        scratch[name] = pltpu.VMEM((ext, cols), BF16)
        scratch[name + "_s"] = dma((5,))
        scratch[name + "_r"] = dma((span + 1,))
    for name in ("lq", "lk", "lv"):
        scratch[name] = pltpu.VMEM((rows, cols), BF16)
    scratch["fetch"] = dma((len(IN_NAMES),))
    scratch["stat_own"] = pltpu.VMEM((stat_rows, rows), F32)
    scratch["stat"] = pltpu.VMEM((span + 1, stat_rows, rows), F32)
    scratch["stat_s"] = dma((span + 1,))
    scratch["stat_r"] = dma((span + 1,))
    scratch["norm_own"] = pltpu.VMEM((8, rows), F32)
    scratch["norm"] = pltpu.VMEM((hn, 8, rows), F32)
    scratch["norm_s"] = dma((hn,))
    scratch["norm_r"] = dma((hn,))
    scratch["lin_scores"] = pltpu.VMEM((heads, rows, rows), BF16)
    scratch["lin_out"] = pltpu.VMEM((rows, cols), F32)
    scratch["lin_dout"] = pltpu.VMEM((rows, cols), BF16)
    scratch["grad_k"] = pltpu.VMEM((rows, cols), F32)
    scratch["grad_v"] = pltpu.VMEM((rows, cols), F32)
    scratch["s"] = pltpu.VMEM((heads, rows, ext), F32)
    scratch["dp"] = pltpu.VMEM((heads, rows, ext), F32)
    scratch["p_low"] = pltpu.VMEM((heads, rows, ext), BF16)
    scratch["ds_low"] = pltpu.VMEM((heads, rows, ext), BF16)
    names = tuple(name + "_in" for name in IN_NAMES) + OUT_NAMES + tuple(scratch)
    flops = 2 * rows * HD * heads * (8 * ext + 14 * HD)
    vmem = pl.BlockSpec(memory_space=pltpu.VMEM)
    hbm = pl.BlockSpec(memory_space=pltpu.HBM)
    outs = pl.pallas_call(
        partial(kernel, n, hn, owners, span, names),
        out_shape=[jax.ShapeDtypeStruct((rows, cols), BF16)] * len(OUT_NAMES),
        in_specs=[hbm] * len(IN_NAMES),
        out_specs=[vmem] * len(OUT_NAMES),
        scratch_shapes=list(scratch.values()),
        compiler_params=pltpu.CompilerParams(
            collective_id=0, has_side_effects=True, vmem_limit_bytes=60 * 2**20
        ),
        cost_estimate=pl.CostEstimate(
            flops=flops, bytes_accessed=14 * rows * cols * 2, transcendentals=2 * heads * rows * ext
        ),
    )(*arrays)
    shapes = [jax.ShapeDtypeStruct(out.shape, out.dtype) for out in outs]
    return tuple(
        pl.pallas_call(
            write_all,
            out_shape=shapes,
            in_specs=[hbm] * len(OUT_NAMES),
            out_specs=[hbm] * len(OUT_NAMES),
            scratch_shapes=[
                pltpu.VMEM((len(OUT_NAMES), rows, cols), BF16), dma((2 * len(OUT_NAMES),))
            ],
            compiler_params=pltpu.CompilerParams(vmem_limit_bytes=60 * 2**20),
        )(*outs)
    )


def solution(mesh):
    split = P("ctx", "head")
    return jax.shard_map(
        partial(shards, mesh.shape["ctx"], mesh.shape["head"]),
        mesh=mesh,
        in_specs=(split,) * len(IN_NAMES),
        out_specs=(split,) * len(OUT_NAMES),
        check_vma=False,
    )
```
